512 devices in a mesh: row: 32 (over z_lo, y, core), col: 16 (over z_hi, x).
Axes of the slice: x: 4, y: 8, z: 8 (z_hi: 4, z_lo: 2; z = z_hi * 2 + z_lo), core: 2. Of those that a mesh axis runs over, the one named last changes fastest.
Arguments:
- tokens: bfloat16 [512, 12288], P('col', 'row'), may hold values from -6 to 6
- weight: bfloat16 [12288, 24576], P('row', 'col'), may hold values from -0.0546875 to 0.0546875
- bias: float32 [24576], P('col'), may hold values from -3 to 3
- cotangent: bfloat16 [512, 24576], P('row', 'col'), may hold values from -6 to 6
Outputs:
- activated: bfloat16 [512, 24576], P('row', 'col')
- grad_tokens: bfloat16 [512, 12288], P('col', 'row')
- grad_weight: bfloat16 [12288, 24576], P('row', 'col')
- grad_bias: float32 [24576], P('col')
The draws below stay inside these ranges and needn't reach their ends.
All inputs are finite; a program needn't handle non-finite values.
Results may differ from the reference program's by a relative error of at most 0.007.
Values may be sent and summed in bfloat16 or wider, within the bound.
A program may use at most 64 MiB of HBM per device.

```python
import jax
import jax.numpy as jnp

D = 12288
FFW = 24576
TOKENS = 512


def levels(rng, shape, shards, smallest, largest):
    level = 1.0
    for position, shards_of in shards:
        draws = jax.random.uniform(jax.random.fold_in(jax.random.fold_in(rng, 6), position), (shards_of,), jnp.float32, smallest / len(shards), largest / len(shards))
        level = level * jnp.repeat(jnp.exp(draws), shape[position] // shards_of).reshape((-1,) + (1,) * (len(shape) - 1 - position))
    return level


def noise(key, dims, scale, most, cuts=(), dtype=jnp.bfloat16):
    result = scale * jax.random.normal(key, dims, jnp.float32)
    if cuts:
        result = result * levels(key, dims, cuts, -0.22, 0.18)
    return jnp.clip(result, -most, most).astype(dtype)


def setup_inputs(seed: int = 0) -> dict:
    key_list = jax.random.split(jax.random.key(seed), 5)
    tokens = noise(key_list[0], (TOKENS, D), 1.0, 6.0, ((0, 16), (1, 32)))
    weight = noise(key_list[1], (D, FFW), D ** -0.5, 0.0546875, ((0, 32), (1, 16)))
    bias = noise(key_list[2], (FFW,), 0.5, 3.0, ((0, 16),), jnp.float32)
    cotangent = noise(key_list[3], (TOKENS, FFW), 1.0, 6.0, ((0, 32), (1, 16)))
    return {"tokens": tokens, "weight": weight, "bias": bias, "cotangent": cotangent}


coef = 0.7978845608


def reference(tokens, weight, bias, cotangent):
    projected = jnp.dot(tokens, weight, preferred_element_type=jnp.float32) + bias[None, :]
    cubic = coef * (projected + 0.044715 * projected * projected * projected)
    bent = jnp.tanh(cubic)
    activated = (0.5 * projected * (1.0 + bent)).astype(jnp.bfloat16)
    deriv = 0.5 * (1.0 + bent) + 0.5 * projected * (1.0 - bent * bent) * coef * (1.0 + 0.134145 * projected * projected)
    slope = (cotangent.astype(jnp.float32) * deriv).astype(jnp.bfloat16)
    grad_weight = jnp.dot(tokens.T, slope, preferred_element_type=jnp.float32).astype(jnp.bfloat16)
    grad_tokens = jnp.dot(slope, weight.T, preferred_element_type=jnp.float32).astype(jnp.bfloat16)
    grad_bias = jnp.sum(slope.astype(jnp.float32), axis=0)
    return activated, grad_tokens, grad_weight, grad_bias
```

```python
import jax
import jax.numpy as jnp
from jax import lax
from jax.experimental import pallas as pl
from jax.experimental.pallas import tpu as pltpu
from jax.sharding import PartitionSpec as P

MESH = pl.DeviceIdType.MESH
coef = 0.7978845608
NX, NZH, NY, NZL = 4, 4, 8, 2
R = 16
F = 384
N = 1536
AROUND_X = (0, 1, 3, 2)
AROUND_Y = (1, 7, 2, 6, 3, 5, 4)


def dot(a, b, dims):
    return lax.dot_general(a, b, (dims, ((), ())), preferred_element_type=jnp.float32)


def kernel(
    tok_h, w_h, b_h, cot_h,
    act_h, gt_h, gw_h, gb_h,
    w2, tok, tokx, cot, bias,
    pown, zsend, zrecv, ysend, yrecv, sl,
    gown, gsend, g1recv, g2send, g2recv,
    actv, gtv, gwv, gbv,
    loc, wsem, a0s, a1s, a1r, a2s, a2r, xsem, zs, zr, ys, yr, es, ezs, er, hs, g1s, g1r, g2s, g2r,
):
    row, col = lax.axis_index("row"), lax.axis_index("col")
    core, y, zl = lax.rem(row, 2), lax.rem(lax.div(row, 2), NY), lax.div(row, 2 * NY)
    x, zh = lax.rem(col, NX), lax.div(col, NX)
    other = 1 - core

    def device(zl_=zl, y_=y, core_=core, zh_=zh, x_=x):
        return {"row": zl_ * (2 * NY) + y_ * 2 + core_, "col": zh_ * NX + x_}

    started = []

    def send(src, dst, ssem, rsem, to):
        copy = pltpu.make_async_remote_copy(
            src_ref=src, dst_ref=dst, send_sem=ssem, recv_sem=rsem, device_id=to, device_id_type=MESH
        )
        copy.start()
        return copy

    def arrived(dst, sem):
        pltpu.make_async_copy(dst, dst, sem).wait()

    w_in = pltpu.make_async_copy(w_h, w2.at[core], loc.at[0])
    tok_in = pltpu.make_async_copy(tok_h.at[pl.ds(core * R, R)], tok.at[x, core, zh], loc.at[1])
    cot_in = pltpu.make_async_copy(cot_h, cot, loc.at[2])
    b_in = pltpu.make_async_copy(b_h, bias, loc.at[3])
    for copy in (tok_in, w_in, cot_in, b_in):
        copy.start()

    barrier = pltpu.get_barrier_semaphore()
    partners = [device(core_=other), device(zl_=1 - zl)]
    partners += [device(y_=lax.rem(y + d, NY)) for d in range(1, NY)]
    partners += [device(x_=lax.rem(x + d, NX)) for d in range(1, NX)]
    partners += [device(zh_=lax.rem(zh + d, NZH), core_=h) for d in range(1, NZH) for h in range(2)]
    for p in partners:
        pl.semaphore_signal(barrier, inc=1, device_id=p, device_id_type=MESH)
    pl.semaphore_wait(barrier, len(partners))

    started.append(
        send(tok_h.at[pl.ds(other * R, R)], tok.at[x, core, zh], a0s, a1r.at[zh, core], device(core_=other))
    )
    for d in (1, 3, 2):
        to = lax.rem(zh + d, NZH)
        for h in range(2):
            started.append(
                send(tok_h.at[pl.ds(h * R, R)], tok.at[x, core, zh], a1s.at[d, h], a1r.at[zh, core], device(zh_=to, core_=h))
            )
    started.append(send(w_h, w2.at[core], wsem.at[0], wsem.at[1], device(core_=other)))

    def spread(z, d):
        for e in (1, 3, 2):
            piece = tok.at[x, :, z]
            started.append(send(piece, piece, a2s.at[d, e], a2r.at[x, z], device(x_=lax.rem(x + e, NX))))

    tok_in.wait()
    arrived(tok.at[x, other, zh], a1r.at[zh, other])
    spread(zh, 0)
    for d in (1, 3, 2):
        z = lax.rem(zh + d, NZH)
        for f in range(2):
            arrived(tok.at[x, f, z], a1r.at[z, f])
        spread(z, d)
    w_in.wait()
    arrived(w2.at[other], wsem.at[1])

    for d in AROUND_X:
        g = lax.rem(x + d, NX)
        if d:
            for z in range(NZH):
                arrived(tok.at[g, :, z], a2r.at[g, z])
        p = dot(tok[g, 0].reshape(NZH * R, F), w2[0], ((1,), (0,)))
        p += dot(tok[g, 1].reshape(NZH * R, F), w2[1], ((1,), (0,)))
        p = p.reshape(NZH, R, N)
        zsend[g] = p.astype(jnp.bfloat16)
        pown[g] = p
        started.append(
            send(zsend.at[g, pl.ds(2 * (1 - zl), 2)], zrecv.at[g], zs.at[d], zr.at[g], device(zl_=1 - zl))
        )
    started.append(send(tok.at[:, other], tokx, xsem.at[0], xsem.at[1], device(core_=other)))

    def ycopy(g, j, d):
        return pltpu.make_async_remote_copy(
            src_ref=ysend.at[g, j], dst_ref=yrecv.at[y], send_sem=ys.at[d, j], recv_sem=yr.at[y],
            device_id=device(y_=j * NX + g), device_id_type=MESH,
        )

    for d in AROUND_X:
        g = lax.rem(x + d, NX)
        arrived(zrecv.at[g], zr.at[g])
        for j in range(2):
            ysend[g, j] = (pown[g, 2 * zl + j] + zrecv[g, j].astype(jnp.float32)).astype(jnp.bfloat16)

            @pl.when(j * NX + g != y)
            def _(g=g, j=j, d=d):
                ycopy(g, j, d).start()

    cot_in.wait()
    b_in.wait()
    yx, yz = lax.rem(y, NX), lax.div(y, NX)
    v = pown[yx, 2 * zl + yz] + zrecv[yx, yz].astype(jnp.float32)
    for d in AROUND_Y:
        s = lax.rem(y + d, NY)
        arrived(yrecv.at[s], yr.at[s])
        v += yrecv[s].astype(jnp.float32)

    v += bias[...].reshape(1, N)
    bent = jnp.tanh(coef * (v + 0.044715 * v * v * v))
    actv[...] = (0.5 * v * (1.0 + bent)).astype(jnp.bfloat16)
    deriv = 0.5 * (1.0 + bent) + 0.5 * v * (1.0 - bent * bent) * coef * (1.0 + 0.134145 * v * v)
    mine = 2 * zl + yz
    sl[core, yx, mine] = (cot[...].astype(jnp.float32) * deriv).astype(jnp.bfloat16)

    def slopes(zl_, y_):
        return sl.at[core, lax.rem(y_, NX), 2 * zl_ + lax.div(y_, NX)]

    own = slopes(zl, y)
    for d in AROUND_Y:
        started.append(send(own, own, es.at[d], er.at[zl, y], device(y_=lax.rem(y + d, NY))))
    started.append(send(own, own, ezs.at[0], er.at[zl, y], device(zl_=1 - zl)))
    act_out = pltpu.make_async_copy(actv, act_h, loc.at[1])
    act_out.start()
    for d in AROUND_Y:
        s = lax.rem(y + d, NY)
        piece = slopes(zl, s)
        arrived(piece, er.at[zl, s])
        started.append(send(piece, piece, ezs.at[d], er.at[zl, s], device(zl_=1 - zl)))

    def g1copy(g, d):
        return pltpu.make_async_remote_copy(
            src_ref=gsend.at[g], dst_ref=g1recv.at[x], send_sem=g1s.at[d], recv_sem=g1r.at[x],
            device_id=device(x_=g), device_id_type=MESH,
        )

    for d in (2, 1, 3, 0):
        g = lax.rem(y + d, NX)
        for j in range(2):
            s = j * NX + g
            arrived(slopes(1 - zl, s), er.at[1 - zl, s])
        a = sl[core, g].reshape(NZH * R, N)
        for f in range(2):
            p = dot(a, w2[f], ((1,), (1,))).reshape(NZH, R, F)
            gsend[g, :, f] = p.astype(jnp.bfloat16)
            gown[g, :, f] = p

        @pl.when(g != x)
        def _(g=g, d=d):
            g1copy(g, d).start()

    started.append(send(sl.at[core], sl.at[core], hs.at[0], hs.at[1], device(core_=other)))

    tiles = 3
    wide = N // tiles
    arrived(tokx, xsem.at[1])
    arrived(sl.at[other], hs.at[1])
    mine_t = tok[:, core].reshape(NX * NZH * R, F)
    other_t = tokx[...].reshape(NX * NZH * R, F)
    for t in range(tiles):
        cut = pl.ds(t * wide, wide)
        p = dot(mine_t, sl[core, :, :, :, cut].reshape(NX * NZH * R, wide), ((0,), (0,)))
        p += dot(other_t, sl[other, :, :, :, cut].reshape(NX * NZH * R, wide), ((0,), (0,)))
        gwv[:, cut] = p.astype(jnp.bfloat16)
    gw_out = pltpu.make_async_copy(gwv, gw_h, loc.at[0])
    gw_out.start()

    def add_bias(i, total):
        return total + sl[i // 16, i // 4 % 4, i % 4].astype(jnp.float32)

    total = lax.fori_loop(0, 32, add_bias, jnp.zeros((R, N), jnp.float32))
    gbv[...] = jnp.sum(total, axis=0)
    gb_out = pltpu.make_async_copy(gbv, gb_h, loc.at[2])
    gb_out.start()

    for d in (1, 3, 2):
        s = lax.rem(x + d, NX)
        arrived(g1recv.at[s], g1r.at[s])
        gown[x] += g1recv[s].astype(jnp.float32)
    g2send[...] = gown[x].astype(jnp.bfloat16)
    for d in (1, 3, 2):
        to = lax.rem(zh + d, NZH)
        for f in range(2):
            started.append(
                send(g2send.at[to, f], g2recv.at[zh, core], g2s.at[d, f], g2r.at[zh, core], device(zh_=to, core_=f))
            )
    started.append(
        send(g2send.at[zh, other], g2recv.at[zh, core], g2s.at[0, 0], g2r.at[zh, core], device(core_=other))
    )
    same = gown[x, zh, core]
    arrived(g2recv.at[zh, other], g2r.at[zh, other])
    cross = g2recv[zh, other].astype(jnp.float32)
    for d in (1, 3, 2):
        s = lax.rem(zh + d, NZH)
        arrived(g2recv.at[s, core], g2r.at[s, core])
        same += g2recv[s, core].astype(jnp.float32)
        arrived(g2recv.at[s, other], g2r.at[s, other])
        cross += g2recv[s, other].astype(jnp.float32)
    gtv[core] = same.astype(jnp.bfloat16)
    gtv[other] = cross.astype(jnp.bfloat16)
    outs = [pltpu.make_async_copy(gtv.at[h], gt_h.at[pl.ds(h * R, R)], loc.at[3 + h]) for h in range(2)]
    for copy in outs:
        copy.start()

    for copy in started:
        copy.wait_send()
    for d in range(NX):
        g = lax.rem(x + d, NX)
        for j in range(2):

            @pl.when(j * NX + g != y)
            def _(g=g, j=j, d=d):
                ycopy(g, j, d).wait_send()

        h = lax.rem(y + d, NX)

        @pl.when(h != x)
        def _(h=h, d=d):
            g1copy(h, d).wait_send()

    for copy in (act_out, gw_out, gb_out, *outs):
        copy.wait()


def body(tokens, weight, bias, cotangent):
    bf, f32 = jnp.bfloat16, jnp.float32
    vmem, dma = pltpu.VMEM, pltpu.SemaphoreType.DMA
    scratch = [
        vmem((2, F, N), bf),
        vmem((NX, 2, NZH, R, F), bf),
        vmem((NX, NZH, R, F), bf),
        vmem((R, N), bf),
        vmem((N,), f32),
        vmem((NX, NZH, R, N), f32),
        vmem((NX, NZH, R, N), bf),
        vmem((NX, 2, R, N), bf),
        vmem((NX, 2, R, N), bf),
        vmem((NY, R, N), bf),
        vmem((2, NX, NZH, R, N), bf),
        vmem((NX, NZH, 2, R, F), f32),
        vmem((NX, NZH, 2, R, F), bf),
        vmem((NX, NZH, 2, R, F), bf),
        vmem((NZH, 2, R, F), bf),
        vmem((NZH, 2, R, F), bf),
        vmem((R, N), bf),
        vmem((2, R, F), bf),
        vmem((F, N), bf),
        vmem((N,), f32),
        dma((5,)),
        dma((2,)),
        dma,
        dma((NZH, 2)),
        dma((NZH, 2)),
        dma((NZH, NX)),
        dma((NX, NZH)),
        dma((2,)),
        dma((NX,)),
        dma((NX,)),
        dma((NX, 2)),
        dma((NY,)),
        dma((NY,)),
        dma((NY,)),
        dma((NZL, NY)),
        dma((2,)),
        dma((NX,)),
        dma((NX,)),
        dma((NZH, 2)),
        dma((NZH, 2)),
    ]
    shapes = [((R, N), bf), ((2 * R, F), bf), ((F, N), bf), ((N,), f32)]
    return pl.pallas_call(
        kernel,
        out_shape=[jax.ShapeDtypeStruct(s, t) for s, t in shapes],
        in_specs=[pl.BlockSpec(memory_space=pl.ANY)] * 4,
        out_specs=[pl.BlockSpec(memory_space=pl.ANY)] * 4,
        scratch_shapes=scratch,
        compiler_params=pltpu.CompilerParams(
            collective_id=0, has_side_effects=True, vmem_limit_bytes=40 << 20
        ),
    )(tokens, weight, bias, cotangent)


def solution(mesh):
    in_specs = (P("col", "row"), P("row", "col"), P("col"), P("row", "col"))
    out_specs = (P("row", "col"), P("col", "row"), P("row", "col"), P("col"))
    return jax.shard_map(body, mesh=mesh, in_specs=in_specs, out_specs=out_specs, check_vma=False)
```

```python
import jax
import jax.numpy as jnp
from jax import lax
from jax.experimental import pallas as pl
from jax.experimental.pallas import tpu as pltpu
from jax.sharding import PartitionSpec as P

MESH = pl.DeviceIdType.MESH
coef = 0.7978845608
NX, NZH, NY, NZL = 4, 4, 8, 2
R = 16
F = 384
N = 1536
AROUND_X = (0, 1, 3, 2)
AROUND_Y = (1, 7, 2, 6, 3, 5, 4)


def dot(a, b, dims):
    return lax.dot_general(a, b, (dims, ((), ())), preferred_element_type=jnp.float32)


def kernel(
    tok_h, w_h, b_h, cot_h,
    act_h, gt_h, gw_h, gb_h,
    w2, wt, tok, tokx, cot, bias,
    pown, zsend, zrecv, ysend, yrecv, sl,
    gown, gsend, g1recv, g2send, g2recv,
    actv, gtv, gwv, gbv,
    loc, wsem, a0s, a1s, a1r, a2s, a2r, xsem, zs, zr, ys, yr, es, ezs, er, hs, g1s, g1r, g2s, g2r,
):
    row, col = lax.axis_index("row"), lax.axis_index("col")
    core, y, zl = lax.rem(row, 2), lax.rem(lax.div(row, 2), NY), lax.div(row, 2 * NY)
    x, zh = lax.rem(col, NX), lax.div(col, NX)
    other = 1 - core

    def device(zl_=zl, y_=y, core_=core, zh_=zh, x_=x):
        return {"row": zl_ * (2 * NY) + y_ * 2 + core_, "col": zh_ * NX + x_}

    started = []

    def send(src, dst, ssem, rsem, to):
        copy = pltpu.make_async_remote_copy(
            src_ref=src, dst_ref=dst, send_sem=ssem, recv_sem=rsem, device_id=to, device_id_type=MESH
        )
        copy.start()
        return copy

    def arrived(dst, sem):
        pltpu.make_async_copy(dst, dst, sem).wait()

    w_in = pltpu.make_async_copy(w_h, w2.at[core], loc.at[0])
    tok_in = pltpu.make_async_copy(tok_h.at[pl.ds(core * R, R)], tok.at[x, core, zh], loc.at[1])
    cot_in = pltpu.make_async_copy(cot_h, cot, loc.at[2])
    b_in = pltpu.make_async_copy(b_h, bias, loc.at[3])
    for copy in (tok_in, w_in, cot_in, b_in):
        copy.start()

    barrier = pltpu.get_barrier_semaphore()
    partners = [device(core_=other), device(zl_=1 - zl)]
    partners += [device(y_=lax.rem(y + d, NY)) for d in range(1, NY)]
    partners += [device(x_=lax.rem(x + d, NX)) for d in range(1, NX)]
    partners += [device(zh_=lax.rem(zh + d, NZH), core_=h) for d in range(1, NZH) for h in range(2)]
    for p in partners:
        pl.semaphore_signal(barrier, inc=1, device_id=p, device_id_type=MESH)
    pl.semaphore_wait(barrier, len(partners))

    started.append(
        send(tok_h.at[pl.ds(other * R, R)], tok.at[x, core, zh], a0s, a1r.at[zh, core], device(core_=other))
    )
    for d in (1, 3, 2):
        to = lax.rem(zh + d, NZH)
        for h in range(2):
            started.append(
                send(tok_h.at[pl.ds(h * R, R)], tok.at[x, core, zh], a1s.at[d, h], a1r.at[zh, core], device(zh_=to, core_=h))
            )
    started.append(send(w_h, w2.at[core], wsem.at[0], wsem.at[1], device(core_=other)))

    def spread(z, d, es):
        for e in es:
            piece = tok.at[x, :, z]
            started.append(send(piece, piece, a2s.at[d, e], a2r.at[x, z], device(x_=lax.rem(x + e, NX))))

    tok_in.wait()
    arrived(tok.at[x, other, zh], a1r.at[zh, other])
    spread(zh, 0, (1, 3))
    for d in (1, 3, 2):
        z = lax.rem(zh + d, NZH)
        for f in range(2):
            arrived(tok.at[x, f, z], a1r.at[z, f])
        spread(z, d, (1, 3))
    w_in.wait()
    arrived(w2.at[other], wsem.at[1])

    for d in AROUND_X:
        g = lax.rem(x + d, NX)
        if d == 1:
            for e in range(NZH):
                spread(lax.rem(zh + e, NZH), e, (2,))
        if d:
            for z in range(NZH):
                arrived(tok.at[g, :, z], a2r.at[g, z])
        p = dot(tok[g, 0].reshape(NZH * R, F), w2[0], ((1,), (0,)))
        p += dot(tok[g, 1].reshape(NZH * R, F), w2[1], ((1,), (0,)))
        p = p.reshape(NZH, R, N)
        zsend[g] = p.astype(jnp.bfloat16)
        pown[g] = p
        started.append(
            send(zsend.at[g, pl.ds(2 * (1 - zl), 2)], zrecv.at[g], zs.at[d], zr.at[g], device(zl_=1 - zl))
        )
    started.append(send(tok.at[:, other], tokx, xsem.at[0], xsem.at[1], device(core_=other)))

    for f in range(2):
        wt[f] = w2[f].T

    def ycopy(g, j, d):
        return pltpu.make_async_remote_copy(
            src_ref=ysend.at[g, j], dst_ref=yrecv.at[y], send_sem=ys.at[d, j], recv_sem=yr.at[y],
            device_id=device(y_=j * NX + g), device_id_type=MESH,
        )

    for d in AROUND_X:
        g = lax.rem(x + d, NX)
        arrived(zrecv.at[g], zr.at[g])
        for j in range(2):
            ysend[g, j] = (pown[g, 2 * zl + j] + zrecv[g, j].astype(jnp.float32)).astype(jnp.bfloat16)

            @pl.when(j * NX + g != y)
            def _(g=g, j=j, d=d):
                ycopy(g, j, d).start()

    cot_in.wait()
    b_in.wait()
    yx, yz = lax.rem(y, NX), lax.div(y, NX)
    v = pown[yx, 2 * zl + yz] + zrecv[yx, yz].astype(jnp.float32)
    for d in AROUND_Y:
        s = lax.rem(y + d, NY)
        arrived(yrecv.at[s], yr.at[s])
        v += yrecv[s].astype(jnp.float32)

    v += bias[...].reshape(1, N)
    bent = jnp.tanh(coef * (v + 0.044715 * v * v * v))
    actv[...] = (0.5 * v * (1.0 + bent)).astype(jnp.bfloat16)
    deriv = 0.5 * (1.0 + bent) + 0.5 * v * (1.0 - bent * bent) * coef * (1.0 + 0.134145 * v * v)
    mine = 2 * zl + yz
    sl[core, yx, mine] = (cot[...].astype(jnp.float32) * deriv).astype(jnp.bfloat16)

    def slopes(zl_, y_):
        return sl.at[core, lax.rem(y_, NX), 2 * zl_ + lax.div(y_, NX)]

    own = slopes(zl, y)
    for d in AROUND_Y:
        started.append(send(own, own, es.at[d], er.at[zl, y], device(y_=lax.rem(y + d, NY))))
    started.append(send(own, own, ezs.at[0], er.at[zl, y], device(zl_=1 - zl)))
    act_out = pltpu.make_async_copy(actv, act_h, loc.at[1])
    act_out.start()
    for d in AROUND_Y:
        s = lax.rem(y + d, NY)
        piece = slopes(zl, s)
        arrived(piece, er.at[zl, s])
        started.append(send(piece, piece, ezs.at[d], er.at[zl, s], device(zl_=1 - zl)))

    def g1copy(g, d):
        return pltpu.make_async_remote_copy(
            src_ref=gsend.at[g], dst_ref=g1recv.at[x], send_sem=g1s.at[d], recv_sem=g1r.at[x],
            device_id=device(x_=g), device_id_type=MESH,
        )

    for d in (2, 1, 3, 0):
        g = lax.rem(y + d, NX)
        for j in range(2):
            s = j * NX + g
            arrived(slopes(1 - zl, s), er.at[1 - zl, s])
        a = sl[core, g].reshape(NZH * R, N)
        for f in range(2):
            p = dot(a, wt[f], ((1,), (0,))).reshape(NZH, R, F)
            gsend[g, :, f] = p.astype(jnp.bfloat16)
            gown[g, :, f] = p

        @pl.when(g != x)
        def _(g=g, d=d):
            g1copy(g, d).start()

    started.append(send(sl.at[core], sl.at[core], hs.at[0], hs.at[1], device(core_=other)))

    tiles = 3
    wide = N // tiles
    arrived(tokx, xsem.at[1])
    arrived(sl.at[other], hs.at[1])
    mine_t = tok[:, core].reshape(NX * NZH * R, F)
    other_t = tokx[...].reshape(NX * NZH * R, F)
    for t in range(tiles):
        cut = pl.ds(t * wide, wide)
        p = dot(mine_t, sl[core, :, :, :, cut].reshape(NX * NZH * R, wide), ((0,), (0,)))
        p += dot(other_t, sl[other, :, :, :, cut].reshape(NX * NZH * R, wide), ((0,), (0,)))
        gwv[:, cut] = p.astype(jnp.bfloat16)
    gw_out = pltpu.make_async_copy(gwv, gw_h, loc.at[0])
    gw_out.start()

    def add_bias(i, total):
        return total + sl[i // 16, i // 4 % 4, i % 4].astype(jnp.float32)

    total = lax.fori_loop(0, 32, add_bias, jnp.zeros((R, N), jnp.float32))
    gbv[...] = jnp.sum(total, axis=0)
    gb_out = pltpu.make_async_copy(gbv, gb_h, loc.at[2])
    gb_out.start()

    for d in (1, 3, 2):
        s = lax.rem(x + d, NX)
        arrived(g1recv.at[s], g1r.at[s])
        gown[x] += g1recv[s].astype(jnp.float32)
    g2send[...] = gown[x].astype(jnp.bfloat16)
    for d in (1, 3, 2):
        to = lax.rem(zh + d, NZH)
        for f in range(2):
            started.append(
                send(g2send.at[to, f], g2recv.at[zh, core], g2s.at[d, f], g2r.at[zh, core], device(zh_=to, core_=f))
            )
    started.append(
        send(g2send.at[zh, other], g2recv.at[zh, core], g2s.at[0, 0], g2r.at[zh, core], device(core_=other))
    )
    same = gown[x, zh, core]
    arrived(g2recv.at[zh, other], g2r.at[zh, other])
    cross = g2recv[zh, other].astype(jnp.float32)
    for d in (1, 3, 2):
        s = lax.rem(zh + d, NZH)
        arrived(g2recv.at[s, core], g2r.at[s, core])
        same += g2recv[s, core].astype(jnp.float32)
        arrived(g2recv.at[s, other], g2r.at[s, other])
        cross += g2recv[s, other].astype(jnp.float32)
    gtv[core] = same.astype(jnp.bfloat16)
    gtv[other] = cross.astype(jnp.bfloat16)
    outs = [pltpu.make_async_copy(gtv.at[h], gt_h.at[pl.ds(h * R, R)], loc.at[3 + h]) for h in range(2)]
    for copy in outs:
        copy.start()

    for copy in started:
        copy.wait_send()
    for d in range(NX):
        g = lax.rem(x + d, NX)
        for j in range(2):

            @pl.when(j * NX + g != y)
            def _(g=g, j=j, d=d):
                ycopy(g, j, d).wait_send()

        h = lax.rem(y + d, NX)

        @pl.when(h != x)
        def _(h=h, d=d):
            g1copy(h, d).wait_send()

    for copy in (act_out, gw_out, gb_out, *outs):
        copy.wait()


def deliver(*refs):
    sems = refs[8]
    copies = [pltpu.make_async_copy(refs[i], refs[4 + i], sems.at[i]) for i in range(4)]
    for copy in copies:
        copy.start()
    for copy in copies:
        copy.wait()


def body(tokens, weight, bias, cotangent):
    bf, f32 = jnp.bfloat16, jnp.float32
    vmem, dma = pltpu.VMEM, pltpu.SemaphoreType.DMA
    scratch = [
        vmem((2, F, N), bf),
        vmem((2, N, F), bf),
        vmem((NX, 2, NZH, R, F), bf),
        vmem((NX, NZH, R, F), bf),
        vmem((R, N), bf),
        vmem((N,), f32),
        vmem((NX, NZH, R, N), f32),
        vmem((NX, NZH, R, N), bf),
        vmem((NX, 2, R, N), bf),
        vmem((NX, 2, R, N), bf),
        vmem((NY, R, N), bf),
        vmem((2, NX, NZH, R, N), bf),
        vmem((NX, NZH, 2, R, F), f32),
        vmem((NX, NZH, 2, R, F), bf),
        vmem((NX, NZH, 2, R, F), bf),
        vmem((NZH, 2, R, F), bf),
        vmem((NZH, 2, R, F), bf),
        vmem((R, N), bf),
        vmem((2, R, F), bf),
        vmem((F, N), bf),
        vmem((N,), f32),
        dma((5,)),
        dma((2,)),
        dma,
        dma((NZH, 2)),
        dma((NZH, 2)),
        dma((NZH, NX)),
        dma((NX, NZH)),
        dma((2,)),
        dma((NX,)),
        dma((NX,)),
        dma((NX, 2)),
        dma((NY,)),
        dma((NY,)),
        dma((NY,)),
        dma((NZL, NY)),
        dma((2,)),
        dma((NX,)),
        dma((NX,)),
        dma((NZH, 2)),
        dma((NZH, 2)),
    ]
    results = [((R, N), bf), ((2 * R, F), bf), ((F, N), bf), ((N,), f32)]
    shapes = [jax.ShapeDtypeStruct(s, t) for s, t in results]
    outs = pl.pallas_call(
        kernel,
        out_shape=shapes,
        in_specs=[pl.BlockSpec(memory_space=pltpu.HBM)] * 4,
        out_specs=[pl.BlockSpec(memory_space=pl.ANY)] * 4,
        scratch_shapes=scratch,
        compiler_params=pltpu.CompilerParams(
            collective_id=0, has_side_effects=True, vmem_limit_bytes=60 << 20
        ),
    )(tokens, weight, bias, cotangent)
    return pl.pallas_call(
        deliver,
        out_shape=shapes,
        in_specs=[pl.BlockSpec(memory_space=pl.ANY)] * 4,
        out_specs=[pl.BlockSpec(memory_space=pltpu.HBM)] * 4,
        scratch_shapes=[dma((4,))],
    )(*outs)


def solution(mesh):
    in_specs = (P("col", "row"), P("row", "col"), P("col"), P("row", "col"))
    out_specs = (P("row", "col"), P("col", "row"), P("row", "col"), P("col"))
    return jax.shard_map(body, mesh=mesh, in_specs=in_specs, out_specs=out_specs, check_vma=False)
```

```python
import jax
import jax.numpy as jnp
from jax import lax
from jax.experimental import pallas as pl
from jax.experimental.pallas import tpu as pltpu
from jax.sharding import PartitionSpec as P

MESH = pl.DeviceIdType.MESH
coef = 0.7978845608
NX, NZH, NY, NZL = 4, 4, 8, 2
R = 16
F = 384
N = 1536
HALVES = 2
W = N // HALVES
AROUND_X = (0, 1, 3, 2)
AROUND_Y = (1, 7, 2, 6, 3, 5, 4)


def dot(a, b, dims):
    return lax.dot_general(a, b, (dims, ((), ())), preferred_element_type=jnp.float32)


def kernel(
    tok_h, w_h, b_h, cot_h,
    act, gt, gw, gb,
    w2, wt, tok, tokx, cot, bias,
    pown, zsend, zrecv, ysend, yrecv, sl,
    gown, gsend, g1recv, g2send, g2recv,
    loc, wsem, a0s, a1s, a1r, a2s, a2r, xsem, zs, zr, ys, yr, es, ezs, er, hs, g1s, g1r, g2s, g2r,
):
    row, col = lax.axis_index("row"), lax.axis_index("col")
    core, y, zl = lax.rem(row, 2), lax.rem(lax.div(row, 2), NY), lax.div(row, 2 * NY)
    x, zh = lax.rem(col, NX), lax.div(col, NX)
    other = 1 - core

    def device(zl_=zl, y_=y, core_=core, zh_=zh, x_=x):
        return {"row": zl_ * (2 * NY) + y_ * 2 + core_, "col": zh_ * NX + x_}

    started = []

    def send(src, dst, ssem, rsem, to):
        copy = pltpu.make_async_remote_copy(
            src_ref=src, dst_ref=dst, send_sem=ssem, recv_sem=rsem, device_id=to, device_id_type=MESH
        )
        copy.start()
        return copy

    def arrived(dst, sem):
        pltpu.make_async_copy(dst, dst, sem).wait()

    w_in = pltpu.make_async_copy(w_h, w2.at[core], loc.at[0])
    tok_in = pltpu.make_async_copy(tok_h.at[pl.ds(core * R, R)], tok.at[x, core, zh], loc.at[1])
    cot_in = pltpu.make_async_copy(cot_h, cot, loc.at[2])
    b_in = pltpu.make_async_copy(b_h, bias, loc.at[3])
    for copy in (tok_in, w_in, cot_in, b_in):
        copy.start()

    barrier = pltpu.get_barrier_semaphore()
    partners = [device(core_=other), device(zl_=1 - zl)]
    partners += [device(y_=lax.rem(y + d, NY)) for d in range(1, NY)]
    partners += [device(x_=lax.rem(x + d, NX)) for d in range(1, NX)]
    partners += [device(zh_=lax.rem(zh + d, NZH), core_=h) for d in range(1, NZH) for h in range(2)]
    for p in partners:
        pl.semaphore_signal(barrier, inc=1, device_id=p, device_id_type=MESH)
    pl.semaphore_wait(barrier, len(partners))

    started.append(
        send(tok_h.at[pl.ds(other * R, R)], tok.at[x, core, zh], a0s, a1r.at[zh, core], device(core_=other))
    )
    for d in (1, 3, 2):
        to = lax.rem(zh + d, NZH)
        for h in range(2):
            started.append(
                send(tok_h.at[pl.ds(h * R, R)], tok.at[x, core, zh], a1s.at[d, h], a1r.at[zh, core], device(zh_=to, core_=h))
            )
    started.append(send(w_h, w2.at[core], wsem.at[0], wsem.at[1], device(core_=other)))

    def spread(z, d, es):
        for e in es:
            piece = tok.at[x, :, z]
            started.append(send(piece, piece, a2s.at[d, e], a2r.at[x, z], device(x_=lax.rem(x + e, NX))))

    tok_in.wait()
    arrived(tok.at[x, other, zh], a1r.at[zh, other])
    spread(zh, 0, (1, 3))
    for d in (1, 3, 2):
        z = lax.rem(zh + d, NZH)
        for f in range(2):
            arrived(tok.at[x, f, z], a1r.at[z, f])
        spread(z, d, (1, 3))
    w_in.wait()
    arrived(w2.at[other], wsem.at[1])

    def zcopy(h, g, d):
        return send(
            zsend.at[h, g, pl.ds(2 * (1 - zl), 2)], zrecv.at[h, g], zs.at[h, d], zr.at[h, g], device(zl_=1 - zl)
        )

    for d in AROUND_X:
        g = lax.rem(x + d, NX)
        if d == 1:
            for e in range(NZH):
                spread(lax.rem(zh + e, NZH), e, (2,))
        if d:
            for z in range(NZH):
                arrived(tok.at[g, :, z], a2r.at[g, z])
        p = dot(tok[g, 0].reshape(NZH * R, F), w2[0], ((1,), (0,)))
        p += dot(tok[g, 1].reshape(NZH * R, F), w2[1], ((1,), (0,)))
        p = p.reshape(NZH, R, N)
        for h in range(HALVES):
            q = p[:, :, h * W : (h + 1) * W]
            zsend[h, g] = q.astype(jnp.bfloat16)
            pown[h, g] = q
        started.append(zcopy(0, g, d))
        if d == 0:
            started.append(zcopy(1, g, d))
    started.append(send(tok.at[:, other], tokx, xsem.at[0], xsem.at[1], device(core_=other)))

    def ycopy(h, g, j, d):
        return pltpu.make_async_remote_copy(
            src_ref=ysend.at[h, g, j], dst_ref=yrecv.at[h, y], send_sem=ys.at[h, d, j], recv_sem=yr.at[h, y],
            device_id=device(y_=j * NX + g), device_id_type=MESH,
        )

    for h in range(HALVES):
        for d in AROUND_X:
            g = lax.rem(x + d, NX)
            arrived(zrecv.at[h, g], zr.at[h, g])
            for j in range(2):
                total = pown[h, g, 2 * zl + j] + zrecv[h, g, j].astype(jnp.float32)
                ysend[h, g, j] = total.astype(jnp.bfloat16)

                @pl.when(j * NX + g != y)
                def _(h=h, g=g, j=j, d=d):
                    ycopy(h, g, j, d).start()

            if h == 0 and d:
                started.append(zcopy(1, g, d))
    for f in range(2):
        wt[f] = w2[f].T

    def slopes(h, zl_, y_):
        return sl.at[h, core, lax.rem(y_, NX), 2 * zl_ + lax.div(y_, NX)]

    cot_in.wait()
    b_in.wait()
    yx, yz = lax.rem(y, NX), lax.div(y, NX)
    mine = 2 * zl + yz
    for h in range(HALVES):
        cut = slice(h * W, (h + 1) * W)
        v = pown[h, yx, mine] + zrecv[h, yx, yz].astype(jnp.float32)
        for d in AROUND_Y:
            s = lax.rem(y + d, NY)
            arrived(yrecv.at[h, s], yr.at[h, s])
            v += yrecv[h, s].astype(jnp.float32)

        v += bias[cut].reshape(1, W)
        bent = jnp.tanh(coef * (v + 0.044715 * v * v * v))
        act[:, cut] = (0.5 * v * (1.0 + bent)).astype(jnp.bfloat16)
        deriv = 0.5 * (1.0 + bent) + 0.5 * v * (1.0 - bent * bent) * coef * (1.0 + 0.134145 * v * v)
        sl[h, core, yx, mine] = (cot[:, cut].astype(jnp.float32) * deriv).astype(jnp.bfloat16)
        own = slopes(h, zl, y)
        for d in AROUND_Y:
            started.append(send(own, own, es.at[h, d], er.at[h, zl, y], device(y_=lax.rem(y + d, NY))))
        started.append(send(own, own, ezs.at[h, 0], er.at[h, zl, y], device(zl_=1 - zl)))
    for h in range(HALVES):
        for d in AROUND_Y:
            s = lax.rem(y + d, NY)
            piece = slopes(h, zl, s)
            arrived(piece, er.at[h, zl, s])
            started.append(send(piece, piece, ezs.at[h, d], er.at[h, zl, s], device(zl_=1 - zl)))

    def g1copy(g, d):
        return pltpu.make_async_remote_copy(
            src_ref=gsend.at[g], dst_ref=g1recv.at[x], send_sem=g1s.at[d], recv_sem=g1r.at[x],
            device_id=device(x_=g), device_id_type=MESH,
        )

    for h in range(HALVES):
        for d in (2, 1, 3, 0):
            g = lax.rem(y + d, NX)
            for j in range(2):
                s = j * NX + g
                arrived(slopes(h, 1 - zl, s), er.at[h, 1 - zl, s])
            a = sl[h, core, g].reshape(NZH * R, W)
            for f in range(2):
                p = dot(a, wt[f, h * W : (h + 1) * W], ((1,), (0,))).reshape(NZH, R, F)
                if h:
                    p += gown[g, :, f]
                gown[g, :, f] = p
                if h == HALVES - 1:
                    gsend[g, :, f] = p.astype(jnp.bfloat16)

            if h == HALVES - 1:

                @pl.when(g != x)
                def _(g=g, d=d):
                    g1copy(g, d).start()

        started.append(send(sl.at[h, core], sl.at[h, core], hs.at[0, h], hs.at[1, h], device(core_=other)))

    arrived(tokx, xsem.at[1])
    mine_t = tok[:, core].reshape(NX * NZH * R, F)
    other_t = tokx[...].reshape(NX * NZH * R, F)
    for h in range(HALVES):
        cut = slice(h * W, (h + 1) * W)
        arrived(sl.at[h, other], hs.at[1, h])
        p = dot(mine_t, sl[h, core].reshape(NX * NZH * R, W), ((0,), (0,)))
        p += dot(other_t, sl[h, other].reshape(NX * NZH * R, W), ((0,), (0,)))
        gw[:, cut] = p.astype(jnp.bfloat16)

        def add_bias(i, total, h=h):
            return total + sl[h, i // 16, i // 4 % 4, i % 4].astype(jnp.float32)

        total = lax.fori_loop(0, 32, add_bias, jnp.zeros((R, W), jnp.float32))
        gb[cut] = jnp.sum(total, axis=0)

    for d in (1, 3, 2):
        s = lax.rem(x + d, NX)
        arrived(g1recv.at[s], g1r.at[s])
        gown[x] += g1recv[s].astype(jnp.float32)
    g2send[...] = gown[x].astype(jnp.bfloat16)
    for d in (1, 3, 2):
        to = lax.rem(zh + d, NZH)
        for f in range(2):
            started.append(
                send(g2send.at[to, f], g2recv.at[zh, core], g2s.at[d, f], g2r.at[zh, core], device(zh_=to, core_=f))
            )
    started.append(
        send(g2send.at[zh, other], g2recv.at[zh, core], g2s.at[0, 0], g2r.at[zh, core], device(core_=other))
    )
    for copy in started[:-7]:
        copy.wait_send()
    for d in range(NX):
        g = lax.rem(x + d, NX)
        for h in range(HALVES):
            for j in range(2):

                @pl.when(j * NX + g != y)
                def _(h=h, g=g, j=j, d=d):
                    ycopy(h, g, j, d).wait_send()

        to = lax.rem(y + d, NX)

        @pl.when(to != x)
        def _(to=to, d=d):
            g1copy(to, d).wait_send()

    same = gown[x, zh, core]
    arrived(g2recv.at[zh, other], g2r.at[zh, other])
    cross = g2recv[zh, other].astype(jnp.float32)
    for d in (1, 3, 2):
        s = lax.rem(zh + d, NZH)
        arrived(g2recv.at[s, core], g2r.at[s, core])
        same += g2recv[s, core].astype(jnp.float32)
        arrived(g2recv.at[s, other], g2r.at[s, other])
        cross += g2recv[s, other].astype(jnp.float32)
    gt[pl.ds(pl.multiple_of(core * R, R), R)] = same.astype(jnp.bfloat16)
    gt[pl.ds(pl.multiple_of(other * R, R), R)] = cross.astype(jnp.bfloat16)
    for copy in started[-7:]:
        copy.wait_send()


def deliver(*refs):
    results, outs, held, sems = refs[:4], refs[4:8], refs[8:12], refs[12]
    into = [pltpu.make_async_copy(results[i], held[i], sems.at[0, i]) for i in range(4)]
    out = [pltpu.make_async_copy(held[i], outs[i], sems.at[1, i]) for i in range(4)]
    for copy in into:
        copy.start()
    for i in (0, 1, 3, 2):
        into[i].wait()
        out[i].start()
    for copy in out:
        copy.wait()


def body(tokens, weight, bias, cotangent):
    bf, f32 = jnp.bfloat16, jnp.float32
    vmem, dma = pltpu.VMEM, pltpu.SemaphoreType.DMA
    scratch = [
        vmem((2, F, N), bf),
        vmem((2, N, F), bf),
        vmem((NX, 2, NZH, R, F), bf),
        vmem((NX, NZH, R, F), bf),
        vmem((R, N), bf),
        vmem((N,), f32),
        vmem((HALVES, NX, NZH, R, W), f32),
        vmem((HALVES, NX, NZH, R, W), bf),
        vmem((HALVES, NX, 2, R, W), bf),
        vmem((HALVES, NX, 2, R, W), bf),
        vmem((HALVES, NY, R, W), bf),
        vmem((HALVES, 2, NX, NZH, R, W), bf),
        vmem((NX, NZH, 2, R, F), f32),
        vmem((NX, NZH, 2, R, F), bf),
        vmem((NX, NZH, 2, R, F), bf),
        vmem((NZH, 2, R, F), bf),
        vmem((NZH, 2, R, F), bf),
        dma((4,)),
        dma((2,)),
        dma,
        dma((NZH, 2)),
        dma((NZH, 2)),
        dma((NZH, NX)),
        dma((NX, NZH)),
        dma((2,)),
        dma((HALVES, NX)),
        dma((HALVES, NX)),
        dma((HALVES, NX, 2)),
        dma((HALVES, NY)),
        dma((HALVES, NY)),
        dma((HALVES, NY)),
        dma((HALVES, NZL, NY)),
        dma((2, HALVES)),
        dma((NX,)),
        dma((NX,)),
        dma((NZH, 2)),
        dma((NZH, 2)),
    ]
    results = [((R, N), bf), ((2 * R, F), bf), ((F, N), bf), ((N,), f32)]
    shapes = [jax.ShapeDtypeStruct(s, t) for s, t in results]
    outs = pl.pallas_call(
        kernel,
        out_shape=shapes,
        in_specs=[pl.BlockSpec(memory_space=pltpu.HBM)] * 4,
        out_specs=[pl.BlockSpec(memory_space=pltpu.VMEM)] * 4,
        scratch_shapes=scratch,
        compiler_params=pltpu.CompilerParams(
            collective_id=0, has_side_effects=True, vmem_limit_bytes=60 << 20
        ),
    )(tokens, weight, bias, cotangent)
    return pl.pallas_call(
        deliver,
        out_shape=shapes,
        in_specs=[pl.BlockSpec(memory_space=pl.ANY)] * 4,
        out_specs=[pl.BlockSpec(memory_space=pl.ANY)] * 4,
        scratch_shapes=[vmem(s, t) for s, t in results] + [dma((2, 4))],
        compiler_params=pltpu.CompilerParams(vmem_limit_bytes=60 << 20),
    )(*outs)


def solution(mesh):
    in_specs = (P("col", "row"), P("row", "col"), P("col"), P("row", "col"))
    out_specs = (P("row", "col"), P("col", "row"), P("row", "col"), P("col"))
    return jax.shard_map(body, mesh=mesh, in_specs=in_specs, out_specs=out_specs, check_vma=False)
```

```python
import jax
import jax.numpy as jnp
from jax import lax
from jax.experimental import pallas as pl
from jax.experimental.pallas import tpu as pltpu
from jax.sharding import PartitionSpec as P

MESH = pl.DeviceIdType.MESH
coef = 0.7978845608
NX, NZH, NY, NZL = 4, 4, 8, 2
R = 16
F = 384
N = 1536
HALVES = 2
W = N // HALVES
AROUND_X = (0, 1, 3, 2)
AROUND_Y = (1, 7, 2, 6, 3, 5, 4)
PAIRS = (2, 1, 3, 0)


def dot(a, b, dims):
    return lax.dot_general(a, b, (dims, ((), ())), preferred_element_type=jnp.float32)


def kernel(
    tok_h, w_h, b_h, cot_h,
    act, gt, gw, gb,
    w2, wt, tok, tokx, cot, bias,
    pown, zsend, zrecv, ysend, yrecv, sl,
    gown, gsend, g1recv, g2send, g2recv, g3recv,
    loc, wsem, a0s, a1s, a1r, a2s, a2r, a3s, a3r, xsem, zs, zr, ys, yr, es, ezs, er, hs, g1s, g1r, g2s, g2r, g3s, g3r,
):
    row, col = lax.axis_index("row"), lax.axis_index("col")
    core, y, zl = lax.rem(row, 2), lax.rem(lax.div(row, 2), NY), lax.div(row, 2 * NY)
    x, zh = lax.rem(col, NX), lax.div(col, NX)
    other = 1 - core

    def device(zl_=zl, y_=y, core_=core, zh_=zh, x_=x):
        return {"row": zl_ * (2 * NY) + y_ * 2 + core_, "col": zh_ * NX + x_}

    started = []

    def send(src, dst, ssem, rsem, to):
        copy = pltpu.make_async_remote_copy(
            src_ref=src, dst_ref=dst, send_sem=ssem, recv_sem=rsem, device_id=to, device_id_type=MESH
        )
        copy.start()
        return copy

    def arrived(dst, sem):
        pltpu.make_async_copy(dst, dst, sem).wait()

    w_in = pltpu.make_async_copy(w_h, w2.at[core], loc.at[0])
    tok_in = pltpu.make_async_copy(tok_h.at[pl.ds(core * R, R)], tok.at[x, core, zh], loc.at[1])
    cot_in = pltpu.make_async_copy(cot_h, cot, loc.at[2])
    b_in = pltpu.make_async_copy(b_h, bias, loc.at[3])
    for copy in (tok_in, w_in, cot_in, b_in):
        copy.start()

    barrier = pltpu.get_barrier_semaphore()
    partners = [device(core_=other), device(zl_=1 - zl)]
    partners += [device(y_=lax.rem(y + d, NY)) for d in range(1, NY)]
    partners += [device(x_=lax.rem(x + d, NX), core_=h) for d in range(1, NX) for h in range(2)]
    partners += [device(zh_=lax.rem(zh + d, NZH), core_=h) for d in range(1, NZH) for h in range(2)]
    for p in partners:
        pl.semaphore_signal(barrier, inc=1, device_id=p, device_id_type=MESH)
    pl.semaphore_wait(barrier, len(partners))

    def share_weight(h):
        cut = pl.ds(h * W, W)
        started.append(send(w_h.at[:, cut], w2.at[core, :, cut], wsem.at[0, h], wsem.at[1, h], device(core_=other)))

    share_weight(0)
    started.append(
        send(tok_h.at[pl.ds(other * R, R)], tok.at[x, core, zh], a0s, a1r.at[zh, core], device(core_=other))
    )
    for d in (1, 3, 2):
        to = lax.rem(zh + d, NZH)
        for h in range(2):
            started.append(
                send(tok_h.at[pl.ds(h * R, R)], tok.at[x, core, zh], a1s.at[d, h], a1r.at[zh, core], device(zh_=to, core_=h))
            )
    for h in range(1, HALVES):
        share_weight(h)
    for e in (1, 3, 2):
        to = lax.rem(x + e, NX)
        for h in range(2):
            started.append(
                send(tok_h.at[pl.ds(h * R, R)], tok.at[x, core, zh], a3s.at[e, h], a3r.at[x, core], device(x_=to, core_=h))
            )

    def spread(z, d, es):
        for e in es:
            piece = tok.at[x, :, z]
            started.append(send(piece, piece, a2s.at[d, e], a2r.at[x, z], device(x_=lax.rem(x + e, NX))))

    tok_in.wait()
    arrived(tok.at[x, other, zh], a1r.at[zh, other])
    for d in (1, 3, 2):
        z = lax.rem(zh + d, NZH)
        for f in range(2):
            arrived(tok.at[x, f, z], a1r.at[z, f])
        spread(z, d, (1, 3, 2))
    w_in.wait()

    def zcopy(h, g, d):
        return send(
            zsend.at[h, g, pl.ds(2 * (1 - zl), 2)], zrecv.at[h, g], zs.at[h, d], zr.at[h, g], device(zl_=1 - zl)
        )

    for d in AROUND_X:
        g = lax.rem(x + d, NX)
        if d:
            for f in range(2):
                arrived(tok.at[g, f, zh], a3r.at[g, f])
            for e in range(1, NZH):
                z = lax.rem(zh + e, NZH)
                arrived(tok.at[g, :, z], a2r.at[g, z])
        for h in range(HALVES):
            cut = slice(h * W, (h + 1) * W)
            if d == 0:
                arrived(w2.at[other, :, pl.ds(h * W, W)], wsem.at[1, h])
            p = dot(tok[g, 0].reshape(NZH * R, F), w2[0, :, cut], ((1,), (0,)))
            p += dot(tok[g, 1].reshape(NZH * R, F), w2[1, :, cut], ((1,), (0,)))
            p = p.reshape(NZH, R, W)
            zsend[h, g] = p.astype(jnp.bfloat16)
            if h == 0 or d == 0:
                started.append(zcopy(h, g, d))
            pown[h, g] = p
    started.append(send(tok.at[:, other], tokx, xsem.at[0], xsem.at[1], device(core_=other)))

    def ycopy(h, g, j, d):
        return pltpu.make_async_remote_copy(
            src_ref=ysend.at[h, g, j], dst_ref=yrecv.at[h, y], send_sem=ys.at[h, d, j], recv_sem=yr.at[h, y],
            device_id=device(y_=j * NX + g), device_id_type=MESH,
        )

    for h in range(HALVES):
        for d in AROUND_X:
            g = lax.rem(x + d, NX)
            arrived(zrecv.at[h, g], zr.at[h, g])
            for j in range(2):
                total = pown[h, g, 2 * zl + j] + zrecv[h, g, j].astype(jnp.float32)
                ysend[h, g, j] = total.astype(jnp.bfloat16)

                @pl.when(j * NX + g != y)
                def _(h=h, g=g, j=j, d=d):
                    ycopy(h, g, j, d).start()

            if h < HALVES - 1 and d:
                started.append(zcopy(h + 1, g, d))
    for f in range(2):
        wt[f] = w2[f].T

    def slopes(h, zl_, y_):
        return sl.at[h, core, lax.rem(y_, NX), 2 * zl_ + lax.div(y_, NX)]

    cot_in.wait()
    b_in.wait()
    yx, yz = lax.rem(y, NX), lax.div(y, NX)
    mine = 2 * zl + yz
    def slope_part(h):
        cut = slice(h * W, (h + 1) * W)
        v = pown[h, yx, mine] + zrecv[h, yx, yz].astype(jnp.float32)
        for d in AROUND_Y:
            s = lax.rem(y + d, NY)
            arrived(yrecv.at[h, s], yr.at[h, s])
            v += yrecv[h, s].astype(jnp.float32)

        v += bias[cut].reshape(1, W)
        bent = jnp.tanh(coef * (v + 0.044715 * v * v * v))
        act[:, cut] = (0.5 * v * (1.0 + bent)).astype(jnp.bfloat16)
        deriv = 0.5 * (1.0 + bent) + 0.5 * v * (1.0 - bent * bent) * coef * (1.0 + 0.134145 * v * v)
        sl[h, core, yx, mine] = (cot[:, cut].astype(jnp.float32) * deriv).astype(jnp.bfloat16)
        started.append(send(slopes(h, zl, y), slopes(h, zl, y), ezs.at[h, 0], er.at[h, zl, y], device(zl_=1 - zl)))

    def partial(h):
        for d in PAIRS:
            g = lax.rem(y + d, NX)
            for j in range(2):
                s = j * NX + g
                arrived(slopes(h, 1 - zl, s), er.at[h, 1 - zl, s])
            a = sl[h, core, g].reshape(NZH * R, W)
            for f in range(2):
                p = dot(a, wt[f, h * W : (h + 1) * W], ((1,), (0,))).reshape(NZH, R, F)
                if h:
                    p += gown[g, :, f]
                gown[g, :, f] = p
                if h == HALVES - 1:
                    q = p.astype(jnp.bfloat16)
                    for z in range(NZH):
                        gsend[g, lax.rem(z - zh + NZH, NZH), f] = q[z]

            if h == HALVES - 1:

                @pl.when(g != x)
                def _(g=g, d=d):
                    g1copy(g, d).start()

    def g1copy(g, d):
        return pltpu.make_async_remote_copy(
            src_ref=gsend.at[g, pl.ds(1, NZH - 1)], dst_ref=g1recv.at[x], send_sem=g1s.at[d], recv_sem=g1r.at[x],
            device_id=device(x_=g), device_id_type=MESH,
        )

    def g3copy(g, d, f):
        return pltpu.make_async_remote_copy(
            src_ref=gsend.at[g, 0, f], dst_ref=g3recv.at[x, core], send_sem=g3s.at[d, f], recv_sem=g3r.at[x, core],
            device_id=device(x_=g, core_=f), device_id_type=MESH,
        )

    for h in range(HALVES):
        slope_part(h)
        own = slopes(h, zl, y)
        for d in AROUND_Y:
            started.append(send(own, own, es.at[h, d], er.at[h, zl, y], device(y_=lax.rem(y + d, NY))))
    for h in range(HALVES):
        for d in AROUND_Y:
            s = lax.rem(y + d, NY)
            piece = slopes(h, zl, s)
            arrived(piece, er.at[h, zl, s])
            started.append(send(piece, piece, ezs.at[h, d], er.at[h, zl, s], device(zl_=1 - zl)))
    for h in range(HALVES):
        partial(h)
        if h == HALVES - 1:
            for d in PAIRS:
                g = lax.rem(y + d, NX)

                @pl.when(g != x)
                def _(g=g, d=d):
                    for f in range(2):
                        g3copy(g, d, f).start()

            started.append(
                send(gsend.at[x, 0, other], g2recv.at[zh, core], g2s.at[0, 0], g2r.at[zh, core], device(core_=other))
            )
        started.append(send(sl.at[h, core], sl.at[h, core], hs.at[0, h], hs.at[1, h], device(core_=other)))

    arrived(tokx, xsem.at[1])
    mine_t = tok[:, core].reshape(NX * NZH * R, F)
    other_t = tokx[...].reshape(NX * NZH * R, F)
    for h in range(HALVES):
        cut = slice(h * W, (h + 1) * W)
        arrived(sl.at[h, other], hs.at[1, h])
        p = dot(mine_t, sl[h, core].reshape(NX * NZH * R, W), ((0,), (0,)))
        p += dot(other_t, sl[h, other].reshape(NX * NZH * R, W), ((0,), (0,)))
        gw[:, cut] = p.astype(jnp.bfloat16)

        def add_bias(i, total, h=h):
            return total + sl[h, i // 16, i // 4 % 4, i % 4].astype(jnp.float32)

        total = lax.fori_loop(0, 32, add_bias, jnp.zeros((R, W), jnp.float32))
        gb[cut] = jnp.sum(total, axis=0)

    for d in (1, 3, 2):
        s = lax.rem(x + d, NX)
        arrived(g1recv.at[s], g1r.at[s])
    final = []
    for d in (2, 1, 3):
        to = lax.rem(zh + d, NZH)
        total = gown[x, to]
        for e in (1, 3, 2):
            total += g1recv[lax.rem(x + e, NX), d - 1].astype(jnp.float32)
        g2send[d] = total.astype(jnp.bfloat16)
        for f in range(2):
            final.append(
                send(g2send.at[d, f], g2recv.at[zh, core], g2s.at[d, f], g2r.at[zh, core], device(zh_=to, core_=f))
            )
    for copy in started:
        copy.wait_send()
    for d in range(NX):
        g = lax.rem(x + d, NX)
        for h in range(HALVES):
            for j in range(2):

                @pl.when(j * NX + g != y)
                def _(h=h, g=g, j=j, d=d):
                    ycopy(h, g, j, d).wait_send()

        to = lax.rem(y + d, NX)

        @pl.when(to != x)
        def _(to=to, d=d):
            g1copy(to, d).wait_send()
            for f in range(2):
                g3copy(to, d, f).wait_send()

    same = gown[x, zh, core]
    arrived(g2recv.at[zh, other], g2r.at[zh, other])
    cross = g2recv[zh, other].astype(jnp.float32)
    for d in (1, 3, 2):
        s = lax.rem(x + d, NX)
        arrived(g3recv.at[s, core], g3r.at[s, core])
        same += g3recv[s, core].astype(jnp.float32)
        arrived(g3recv.at[s, other], g3r.at[s, other])
        cross += g3recv[s, other].astype(jnp.float32)
    for d in (1, 3, 2):
        s = lax.rem(zh + d, NZH)
        arrived(g2recv.at[s, core], g2r.at[s, core])
        same += g2recv[s, core].astype(jnp.float32)
        arrived(g2recv.at[s, other], g2r.at[s, other])
        cross += g2recv[s, other].astype(jnp.float32)
    gt[pl.ds(pl.multiple_of(core * R, R), R)] = same.astype(jnp.bfloat16)
    gt[pl.ds(pl.multiple_of(other * R, R), R)] = cross.astype(jnp.bfloat16)
    for copy in final:
        copy.wait_send()


def body(tokens, weight, bias, cotangent):
    bf, f32 = jnp.bfloat16, jnp.float32
    vmem, dma = pltpu.VMEM, pltpu.SemaphoreType.DMA
    scratch = [
        vmem((2, F, N), bf),
        vmem((2, N, F), bf),
        vmem((NX, 2, NZH, R, F), bf),
        vmem((NX, NZH, R, F), bf),
        vmem((R, N), bf),
        vmem((N,), f32),
        vmem((HALVES, NX, NZH, R, W), f32),
        vmem((HALVES, NX, NZH, R, W), bf),
        vmem((HALVES, NX, 2, R, W), bf),
        vmem((HALVES, NX, 2, R, W), bf),
        vmem((HALVES, NY, R, W), bf),
        vmem((HALVES, 2, NX, NZH, R, W), bf),
        vmem((NX, NZH, 2, R, F), f32),
        vmem((NX, NZH, 2, R, F), bf),
        vmem((NX, NZH - 1, 2, R, F), bf),
        vmem((NZH, 2, R, F), bf),
        vmem((NZH, 2, R, F), bf),
        vmem((NX, 2, R, F), bf),
        dma((4,)),
        dma((2, HALVES)),
        dma,
        dma((NZH, 2)),
        dma((NZH, 2)),
        dma((NZH, NX)),
        dma((NX, NZH)),
        dma((NX, 2)),
        dma((NX, 2)),
        dma((2,)),
        dma((HALVES, NX)),
        dma((HALVES, NX)),
        dma((HALVES, NX, 2)),
        dma((HALVES, NY)),
        dma((HALVES, NY)),
        dma((HALVES, NY)),
        dma((HALVES, NZL, NY)),
        dma((2, HALVES)),
        dma((NX,)),
        dma((NX,)),
        dma((NZH, 2)),
        dma((NZH, 2)),
        dma((NX, 2)),
        dma((NX, 2)),
    ]
    results = [((R, N), bf), ((2 * R, F), bf), ((F, N), bf), ((N,), f32)]
    shapes = [jax.ShapeDtypeStruct(s, t) for s, t in results]
    outs = pl.pallas_call(
        kernel,
        out_shape=[pltpu.VMEM(s, t) for s, t in results],
        in_specs=[pl.BlockSpec(memory_space=pltpu.HBM)] * 4,
        scratch_shapes=scratch,
        compiler_params=pltpu.CompilerParams(
            collective_id=0, has_side_effects=True, vmem_limit_bytes=58 << 20
        ),
    )(tokens, weight, bias, cotangent)
    return outs


def solution(mesh):
    in_specs = (P("col", "row"), P("row", "col"), P("col"), P("row", "col"))
    out_specs = (P("row", "col"), P("col", "row"), P("row", "col"), P("col"))
    return jax.shard_map(body, mesh=mesh, in_specs=in_specs, out_specs=out_specs, check_vma=False)
```

```python
import jax
import jax.numpy as jnp
from jax import lax
from jax.experimental import pallas as pl
from jax.experimental.pallas import tpu as pltpu
from jax.sharding import PartitionSpec as P

MESH = pl.DeviceIdType.MESH
coef = 0.7978845608
NX, NZH, NY, NZL = 4, 4, 8, 2
R = 16
F = 384
N = 1536
HALVES = 2
W = N // HALVES
AROUND_X = (0, 1, 3, 2)
AROUND_Y = (1, 7, 2, 6, 3, 5, 4)
PAIRS = (2, 1, 3, 0)


def dot(a, b, dims):
    return lax.dot_general(a, b, (dims, ((), ())), preferred_element_type=jnp.float32)


def kernel(
    tok_h, w_h, b_h, cot_h,
    act, gt, gw, gb,
    w2, wt, tok, tokx, cot, bias,
    pown, zsend, zrecv, ysend, yrecv, sl,
    gown, gsend, g1recv, g2send, g2recv, g3recv,
    loc, wsem, a0s, a1s, a1r, a2s, a2r, a3s, a3r, xsem, zs, zr, ys, yr, es, ezs, er, hs, g1s, g1r, g2s, g2r, g3s, g3r,
):
    row, col = lax.axis_index("row"), lax.axis_index("col")
    core, y, zl = lax.rem(row, 2), lax.rem(lax.div(row, 2), NY), lax.div(row, 2 * NY)
    x, zh = lax.rem(col, NX), lax.div(col, NX)
    other = 1 - core

    def device(zl_=zl, y_=y, core_=core, zh_=zh, x_=x):
        return {"row": zl_ * (2 * NY) + y_ * 2 + core_, "col": zh_ * NX + x_}

    started = []

    def send(src, dst, ssem, rsem, to):
        copy = pltpu.make_async_remote_copy(
            src_ref=src, dst_ref=dst, send_sem=ssem, recv_sem=rsem, device_id=to, device_id_type=MESH
        )
        copy.start()
        return copy

    def arrived(dst, sem):
        pltpu.make_async_copy(dst, dst, sem).wait()

    w_in = pltpu.make_async_copy(w_h, w2.at[core], loc.at[0])
    tok_in = pltpu.make_async_copy(tok_h.at[pl.ds(core * R, R)], tok.at[x, core, zh], loc.at[1])
    cot_in = pltpu.make_async_copy(cot_h, cot, loc.at[2])
    b_in = pltpu.make_async_copy(b_h, bias, loc.at[3])
    for copy in (tok_in, w_in, cot_in, b_in):
        copy.start()

    barrier = pltpu.get_barrier_semaphore()
    partners = [device(core_=other), device(zl_=1 - zl)]
    partners += [device(y_=lax.rem(y + d, NY)) for d in range(1, NY)]
    partners += [device(x_=lax.rem(x + d, NX), core_=h) for d in range(1, NX) for h in range(2)]
    partners += [device(zh_=lax.rem(zh + d, NZH), core_=h) for d in range(1, NZH) for h in range(2)]
    for p in partners:
        pl.semaphore_signal(barrier, inc=1, device_id=p, device_id_type=MESH)
    pl.semaphore_wait(barrier, len(partners))

    def share_weight(h):
        cut = pl.ds(h * W, W)
        started.append(send(w_h.at[:, cut], w2.at[core, :, cut], wsem.at[0, h], wsem.at[1, h], device(core_=other)))

    share_weight(0)
    started.append(
        send(tok_h.at[pl.ds(other * R, R)], tok.at[x, core, zh], a0s, a1r.at[zh, core], device(core_=other))
    )
    for d in (1, 3, 2):
        to = lax.rem(zh + d, NZH)
        for h in range(2):
            started.append(
                send(tok_h.at[pl.ds(h * R, R)], tok.at[x, core, zh], a1s.at[d, h], a1r.at[zh, core], device(zh_=to, core_=h))
            )
    for h in range(1, HALVES):
        share_weight(h)
    for e in (1, 3, 2):
        to = lax.rem(x + e, NX)
        for h in range(2):
            started.append(
                send(tok_h.at[pl.ds(h * R, R)], tok.at[x, core, zh], a3s.at[e, h], a3r.at[x, core], device(x_=to, core_=h))
            )

    def spread(z, d, es):
        for e in es:
            piece = tok.at[x, :, z]
            started.append(send(piece, piece, a2s.at[d, e], a2r.at[x, z], device(x_=lax.rem(x + e, NX))))

    tok_in.wait()
    arrived(tok.at[x, other, zh], a1r.at[zh, other])
    for d in (1, 3, 2):
        z = lax.rem(zh + d, NZH)
        for f in range(2):
            arrived(tok.at[x, f, z], a1r.at[z, f])
        spread(z, d, (1, 3, 2))
    w_in.wait()

    def zcopy(h, g, d):
        return send(
            zsend.at[h, g, pl.ds(2 * (1 - zl), 2)], zrecv.at[h, g], zs.at[h, d], zr.at[h, g], device(zl_=1 - zl)
        )

    for d in AROUND_X:
        g = lax.rem(x + d, NX)
        if d:
            for f in range(2):
                arrived(tok.at[g, f, zh], a3r.at[g, f])
            for e in range(1, NZH):
                z = lax.rem(zh + e, NZH)
                arrived(tok.at[g, :, z], a2r.at[g, z])
        for h in range(HALVES):
            cut = slice(h * W, (h + 1) * W)
            if d == 0:
                arrived(w2.at[other, :, pl.ds(h * W, W)], wsem.at[1, h])
            p = dot(tok[g, 0].reshape(NZH * R, F), w2[0, :, cut], ((1,), (0,)))
            p += dot(tok[g, 1].reshape(NZH * R, F), w2[1, :, cut], ((1,), (0,)))
            p = p.reshape(NZH, R, W)
            zsend[h, g] = p.astype(jnp.bfloat16)
            if h == 0 or d == 0:
                started.append(zcopy(h, g, d))
            pown[h, g] = p
        if d == 0:
            for f in range(2):
                wt[f] = w2[f].T
    started.append(send(tok.at[:, other], tokx, xsem.at[0], xsem.at[1], device(core_=other)))

    def ycopy(h, g, j, d):
        return pltpu.make_async_remote_copy(
            src_ref=ysend.at[h, g, j], dst_ref=yrecv.at[h, y], send_sem=ys.at[h, d, j], recv_sem=yr.at[h, y],
            device_id=device(y_=j * NX + g), device_id_type=MESH,
        )

    for h in range(HALVES):
        for d in AROUND_X:
            g = lax.rem(x + d, NX)
            arrived(zrecv.at[h, g], zr.at[h, g])
            for j in range(2):
                total = pown[h, g, 2 * zl + j] + zrecv[h, g, j].astype(jnp.float32)
                ysend[h, g, j] = total.astype(jnp.bfloat16)

                @pl.when(j * NX + g != y)
                def _(h=h, g=g, j=j, d=d):
                    ycopy(h, g, j, d).start()

            if h < HALVES - 1 and d:
                started.append(zcopy(h + 1, g, d))
    def slopes(h, zl_, y_):
        return sl.at[h, core, lax.rem(y_, NX), 2 * zl_ + lax.div(y_, NX)]

    cot_in.wait()
    b_in.wait()
    yx, yz = lax.rem(y, NX), lax.div(y, NX)
    mine = 2 * zl + yz
    def slope_part(h):
        cut = slice(h * W, (h + 1) * W)
        v = pown[h, yx, mine] + zrecv[h, yx, yz].astype(jnp.float32)
        for d in AROUND_Y:
            s = lax.rem(y + d, NY)
            arrived(yrecv.at[h, s], yr.at[h, s])
            v += yrecv[h, s].astype(jnp.float32)

        v += bias[cut].reshape(1, W)
        bent = jnp.tanh(coef * (v + 0.044715 * v * v * v))
        act[:, cut] = (0.5 * v * (1.0 + bent)).astype(jnp.bfloat16)
        deriv = 0.5 * (1.0 + bent) + 0.5 * v * (1.0 - bent * bent) * coef * (1.0 + 0.134145 * v * v)
        sl[h, core, yx, mine] = (cot[:, cut].astype(jnp.float32) * deriv).astype(jnp.bfloat16)
        started.append(send(slopes(h, zl, y), slopes(h, zl, y), ezs.at[h, 0], er.at[h, zl, y], device(zl_=1 - zl)))

    def partial(h):
        for d in PAIRS:
            g = lax.rem(y + d, NX)
            for j in range(2):
                s = j * NX + g
                arrived(slopes(h, 1 - zl, s), er.at[h, 1 - zl, s])
            a = sl[h, core, g].reshape(NZH * R, W)
            for f in range(2):
                p = dot(a, wt[f, h * W : (h + 1) * W], ((1,), (0,))).reshape(NZH, R, F)
                if h:
                    p += gown[g, :, f]
                gown[g, :, f] = p
                if h == HALVES - 1:
                    q = p.astype(jnp.bfloat16)
                    for z in range(NZH):
                        gsend[g, lax.rem(z - zh + NZH, NZH), f] = q[z]

            if h == HALVES - 1:

                @pl.when(g != x)
                def _(g=g, d=d):
                    g1copy(g, d).start()

    def g1copy(g, d):
        return pltpu.make_async_remote_copy(
            src_ref=gsend.at[g, pl.ds(1, NZH - 1)], dst_ref=g1recv.at[x], send_sem=g1s.at[d], recv_sem=g1r.at[x],
            device_id=device(x_=g), device_id_type=MESH,
        )

    def g3copy(g, d, f):
        return pltpu.make_async_remote_copy(
            src_ref=gsend.at[g, 0, f], dst_ref=g3recv.at[x, core], send_sem=g3s.at[d, f], recv_sem=g3r.at[x, core],
            device_id=device(x_=g, core_=f), device_id_type=MESH,
        )

    for h in range(HALVES):
        slope_part(h)
        own = slopes(h, zl, y)
        for d in AROUND_Y:
            started.append(send(own, own, es.at[h, d], er.at[h, zl, y], device(y_=lax.rem(y + d, NY))))
    for h in range(HALVES):
        for d in AROUND_Y:
            s = lax.rem(y + d, NY)
            piece = slopes(h, zl, s)
            arrived(piece, er.at[h, zl, s])
            started.append(send(piece, piece, ezs.at[h, d], er.at[h, zl, s], device(zl_=1 - zl)))
    for h in range(HALVES):
        partial(h)
        if h == HALVES - 1:
            for d in PAIRS:
                g = lax.rem(y + d, NX)

                @pl.when(g != x)
                def _(g=g, d=d):
                    for f in range(2):
                        g3copy(g, d, f).start()

            started.append(
                send(gsend.at[x, 0, other], g2recv.at[zh, core], g2s.at[0, 0], g2r.at[zh, core], device(core_=other))
            )
        started.append(send(sl.at[h, core], sl.at[h, core], hs.at[0, h], hs.at[1, h], device(core_=other)))

    arrived(tokx, xsem.at[1])
    mine_t = tok[:, core].reshape(NX * NZH * R, F)
    other_t = tokx[...].reshape(NX * NZH * R, F)
    for h in range(HALVES):
        cut = slice(h * W, (h + 1) * W)
        arrived(sl.at[h, other], hs.at[1, h])
        p = dot(mine_t, sl[h, core].reshape(NX * NZH * R, W), ((0,), (0,)))
        p += dot(other_t, sl[h, other].reshape(NX * NZH * R, W), ((0,), (0,)))
        gw[:, cut] = p.astype(jnp.bfloat16)

        def add_bias(i, total, h=h):
            return total + sl[h, i // 16, i // 4 % 4, i % 4].astype(jnp.float32)

        total = lax.fori_loop(0, 32, add_bias, jnp.zeros((R, W), jnp.float32))
        gb[cut] = jnp.sum(total, axis=0)

    for d in (1, 3, 2):
        s = lax.rem(x + d, NX)
        arrived(g1recv.at[s], g1r.at[s])
    final = []
    for d in (2, 1, 3):
        to = lax.rem(zh + d, NZH)
        total = gown[x, to]
        for e in (1, 3, 2):
            total += g1recv[lax.rem(x + e, NX), d - 1].astype(jnp.float32)
        g2send[d] = total.astype(jnp.bfloat16)
        for f in range(2):
            final.append(
                send(g2send.at[d, f], g2recv.at[zh, core], g2s.at[d, f], g2r.at[zh, core], device(zh_=to, core_=f))
            )
    for copy in started:
        copy.wait_send()
    for d in range(NX):
        g = lax.rem(x + d, NX)
        for h in range(HALVES):
            for j in range(2):

                @pl.when(j * NX + g != y)
                def _(h=h, g=g, j=j, d=d):
                    ycopy(h, g, j, d).wait_send()

        to = lax.rem(y + d, NX)

        @pl.when(to != x)
        def _(to=to, d=d):
            g1copy(to, d).wait_send()
            for f in range(2):
                g3copy(to, d, f).wait_send()

    same = gown[x, zh, core]
    arrived(g2recv.at[zh, other], g2r.at[zh, other])
    cross = g2recv[zh, other].astype(jnp.float32)
    for d in (1, 3, 2):
        s = lax.rem(x + d, NX)
        arrived(g3recv.at[s, core], g3r.at[s, core])
        same += g3recv[s, core].astype(jnp.float32)
        arrived(g3recv.at[s, other], g3r.at[s, other])
        cross += g3recv[s, other].astype(jnp.float32)
    for d in (1, 3, 2):
        s = lax.rem(zh + d, NZH)
        arrived(g2recv.at[s, core], g2r.at[s, core])
        same += g2recv[s, core].astype(jnp.float32)
        arrived(g2recv.at[s, other], g2r.at[s, other])
        cross += g2recv[s, other].astype(jnp.float32)
    gt[pl.ds(pl.multiple_of(core * R, R), R)] = same.astype(jnp.bfloat16)
    gt[pl.ds(pl.multiple_of(other * R, R), R)] = cross.astype(jnp.bfloat16)
    for copy in final:
        copy.wait_send()


def body(tokens, weight, bias, cotangent):
    bf, f32 = jnp.bfloat16, jnp.float32
    vmem, dma = pltpu.VMEM, pltpu.SemaphoreType.DMA
    scratch = [
        vmem((2, F, N), bf),
        vmem((2, N, F), bf),
        vmem((NX, 2, NZH, R, F), bf),
        vmem((NX, NZH, R, F), bf),
        vmem((R, N), bf),
        vmem((N,), f32),
        vmem((HALVES, NX, NZH, R, W), f32),
        vmem((HALVES, NX, NZH, R, W), bf),
        vmem((HALVES, NX, 2, R, W), bf),
        vmem((HALVES, NX, 2, R, W), bf),
        vmem((HALVES, NY, R, W), bf),
        vmem((HALVES, 2, NX, NZH, R, W), bf),
        vmem((NX, NZH, 2, R, F), f32),
        vmem((NX, NZH, 2, R, F), bf),
        vmem((NX, NZH - 1, 2, R, F), bf),
        vmem((NZH, 2, R, F), bf),
        vmem((NZH, 2, R, F), bf),
        vmem((NX, 2, R, F), bf),
        dma((4,)),
        dma((2, HALVES)),
        dma,
        dma((NZH, 2)),
        dma((NZH, 2)),
        dma((NZH, NX)),
        dma((NX, NZH)),
        dma((NX, 2)),
        dma((NX, 2)),
        dma((2,)),
        dma((HALVES, NX)),
        dma((HALVES, NX)),
        dma((HALVES, NX, 2)),
        dma((HALVES, NY)),
        dma((HALVES, NY)),
        dma((HALVES, NY)),
        dma((HALVES, NZL, NY)),
        dma((2, HALVES)),
        dma((NX,)),
        dma((NX,)),
        dma((NZH, 2)),
        dma((NZH, 2)),
        dma((NX, 2)),
        dma((NX, 2)),
    ]
    results = [((R, N), bf), ((2 * R, F), bf), ((F, N), bf), ((N,), f32)]
    shapes = [jax.ShapeDtypeStruct(s, t) for s, t in results]
    outs = pl.pallas_call(
        kernel,
        out_shape=[pltpu.VMEM(s, t) for s, t in results],
        in_specs=[pl.BlockSpec(memory_space=pltpu.HBM)] * 4,
        scratch_shapes=scratch,
        compiler_params=pltpu.CompilerParams(
            collective_id=0, has_side_effects=True, vmem_limit_bytes=58 << 20
        ),
    )(tokens, weight, bias, cotangent)
    return outs


def solution(mesh):
    in_specs = (P("col", "row"), P("row", "col"), P("col"), P("row", "col"))
    out_specs = (P("row", "col"), P("col", "row"), P("row", "col"), P("col"))
    return jax.shard_map(body, mesh=mesh, in_specs=in_specs, out_specs=out_specs, check_vma=False)
```
